512 devices in a mesh: rep: 16 (over x, y_lo), fsdp: 32 (over z, y_hi, core).
Axes of the slice: x: 4, y: 8 (y_hi: 2, y_lo: 4; y = y_hi * 4 + y_lo), z: 8, core: 2. Of those that a mesh axis runs over, the one named last changes fastest.
Arguments:
- tokens: bfloat16 [122880, 4096], P(('rep', 'fsdp')), may hold values from -24 to 24
- norm_gain: bfloat16 [4096], replicated, may hold values from 0.5 to 1.5
- weight: bfloat16 [16, 4096, 512], P('rep', 'fsdp'), may hold values from -6 to 6
- momentum: bfloat16 [16, 4096, 512], P('rep', 'fsdp'), may hold values from -4 to 4
- key_grad: bfloat16 [122880, 512], P(('rep', 'fsdp')), may hold values from -4.1875 to 4.1875
- matching: int32 [16], replicated, may hold values from 0 to 15, as said below
Outputs:
- keys: bfloat16 [122880, 512], P(('rep', 'fsdp'))
- token_grad: bfloat16 [122880, 4096], P(('rep', 'fsdp'))
- new_weight: bfloat16 [16, 4096, 512], P('rep', 'fsdp')
- new_momentum: bfloat16 [16, 4096, 512], P('rep', 'fsdp')
The draws below stay inside these ranges and needn't reach their ends.
Inputs may be any that keep to these rules, and one draw needn't show every extreme that they name: matching is a permutation of the 16 groups.
All inputs are finite; a program needn't handle non-finite values.
Results may differ from the reference program's by a relative error of at most 0.02.
Values may be sent and summed in bfloat16 or wider, within the bound.
No kernel may reach another device: no remote copies, remote signals or barrier semaphores. Data moves between devices by JAX's collectives and lax.ppermute only.
A program may use at most 64 MiB of HBM per device.

```python
import jax
import jax.numpy as jnp
from jax import lax

D = 4096
KEY_WIDTH = 512
TOK_DEV = 240
GROUPS = 16
GROUP_TOKENS = 7680
N_FSDP = 32


def draw_matching(key, part):
    key = jax.random.fold_in(key, 7)
    first_key, second_key = jax.random.split(key)
    order = jax.random.permutation(first_key, GROUPS).astype(jnp.int32)
    anchor = jax.random.randint(second_key, (), 0, GROUPS).astype(jnp.int32)
    target = ((anchor + GROUPS // 2) % GROUPS).astype(jnp.int32)
    current = jnp.sum(jnp.where(jnp.arange(GROUPS) == anchor, order, 0)).astype(jnp.int32)
    order = jnp.where(order == target, current, order)
    order = jnp.where(jnp.arange(GROUPS) == anchor, target, order)
    return order.astype(jnp.int32)


def with_spikes(values, own_key, source, target, shards_of, factor):
    owner, partner = [(jnp.arange(values.shape[position]) // (values.shape[position] // shards_of)).reshape([-1 if axis == position else 1 for axis in range(values.ndim)]) for position in (source, target)]
    chosen = jax.random.permutation(own_key, shards_of)[partner]
    strong = (owner == chosen) | (owner == (partner + shards_of // 2) % shards_of)
    return jnp.where(strong, factor * values, values)


def levels(rng, shape, shards, low, largest):
    def one(dim, parts):
        heights = jax.random.uniform(jax.random.fold_in(jax.random.fold_in(rng, 6), dim), (parts,), jnp.float32, low / len(shards), largest / len(shards))
        return jnp.repeat(jnp.exp(heights), shape[dim] // parts).reshape((-1,) + (1,) * (len(shape) - dim - 1))

    gain = one(*shards[0])
    for cut in shards[1:]:
        gain = gain * one(*cut)
    return gain


def normal_values(own_key, shape, width, limit, cuts=(), dtype=jnp.bfloat16):
    values = width * jax.random.normal(own_key, shape, jnp.float32)
    if cuts:
        values = values * levels(own_key, shape, cuts, -0.22, 0.18)
    return jnp.clip(values, -limit, limit).astype(dtype)


def heavy_noise(key, dims, deviation, limit, shards, heavy, kind=jnp.bfloat16):
    result = deviation * jax.random.normal(key, dims, jnp.float32)
    if shards:
        result = result * levels(key, dims, shards, -0.22, 0.18)
    return jnp.clip(with_spikes(result, jax.random.fold_in(key, 3), *heavy), -limit, limit).astype(kind)


def setup_inputs(seed: int = 0) -> dict:
    key_of = jax.random.split(jax.random.key(seed), 7)
    tokens = heavy_noise(key_of[0], (GROUPS * GROUP_TOKENS, D), 1.0, 24.0, ((0, 512),), (0, 1, 512, 6.0))
    norm_gain = jnp.clip(1.0 + 0.1 * jax.random.normal(key_of[1], (D,), jnp.float32), 0.5, 1.5).astype(jnp.bfloat16)
    weight = normal_values(key_of[2], (GROUPS, D, KEY_WIDTH), 1.0, 6.0, ((0, 16), (1, 32)))
    momentum = normal_values(key_of[3], (GROUPS, D, KEY_WIDTH), 0.5, 4.0, ((0, 16), (1, 32)))
    key_grad = normal_values(key_of[4], (GROUPS * GROUP_TOKENS, KEY_WIDTH), 0.7, 4.1875, ((0, 512),))
    matching = draw_matching(jax.random.fold_in(key_of[6], 71), 0)
    return dict(tokens=tokens, norm_gain=norm_gain, weight=weight, momentum=momentum, key_grad=key_grad, matching=matching)


epsilon = 1e-05
momentum_decay = 0.9
outer_rate = 0.7

def one_group(norm_gain, packed):
    tokens_group, cot_group, weight_group = packed
    width_scale = D ** (-0.5)
    tokens_f = tokens_group.astype(jnp.float32)
    gain_f = norm_gain.astype(jnp.float32)
    inverse_rms = lax.rsqrt(lax.optimization_barrier(jnp.mean(tokens_f * tokens_f, axis=-1, keepdims=True)) + epsilon)
    normed = (tokens_f * inverse_rms * gain_f).astype(jnp.bfloat16)
    keys = (jnp.dot(normed, weight_group, preferred_element_type=jnp.float32) * width_scale).astype(jnp.bfloat16)
    normed_grad = (lax.dot_general(cot_group, weight_group, (((1,), (1,)), ((), ())), preferred_element_type=jnp.float32) * width_scale).astype(jnp.bfloat16)
    upstream = normed_grad.astype(jnp.float32) * gain_f
    mixed = lax.optimization_barrier(jnp.mean(upstream * tokens_f, axis=-1, keepdims=True))
    token_grad = (inverse_rms * (upstream - tokens_f * inverse_rms * inverse_rms * mixed)).astype(jnp.bfloat16)
    blocks_normed = normed.reshape(N_FSDP, TOK_DEV, D)
    blocks_cot = cot_group.reshape(N_FSDP, TOK_DEV, KEY_WIDTH)

    def add_block(total, pair):
        block_n, block_c = pair
        term = (lax.dot_general(block_n, block_c, (((0,), (0,)), ((), ())), preferred_element_type=jnp.float32) * width_scale).astype(jnp.bfloat16)
        term = lax.optimization_barrier(term)
        return (total + term.astype(jnp.float32), None)
    total, _ = lax.scan(add_block, jnp.zeros((D, KEY_WIDTH), jnp.float32), (blocks_normed, blocks_cot))
    return (keys, token_grad, total.astype(jnp.bfloat16))

def reference(tokens, norm_gain, weight, momentum, key_grad, matching):
    tokens_all = tokens.reshape(GROUPS, GROUP_TOKENS, D)
    cot_all = key_grad.reshape(GROUPS, GROUP_TOKENS, KEY_WIDTH)
    keys, token_grad, grad = lax.map(lambda packed: one_group(norm_gain, packed), (tokens_all, cot_all, weight))
    weight_f = weight.astype(jnp.float32)
    momentum_f = momentum.astype(jnp.float32)
    mean_weight = (weight_f + weight_f[matching]) * 0.5
    mean_momentum = (momentum_f + momentum_f[matching]) * 0.5
    grad_f = grad.astype(jnp.float32)
    momentum_next = momentum_decay * mean_momentum + grad_f
    new_weight = (mean_weight - outer_rate * (grad_f + momentum_decay * momentum_next)).astype(jnp.bfloat16)
    new_momentum = momentum_next.astype(jnp.bfloat16)
    return (keys.reshape(GROUPS * GROUP_TOKENS, KEY_WIDTH), token_grad.reshape(GROUPS * GROUP_TOKENS, D), new_weight, new_momentum)
```

```python
import jax
import jax.numpy as jnp
from jax import lax
from jax.experimental import pallas as pl
from jax.experimental.pallas import tpu as pltpu
from jax.sharding import PartitionSpec as P

epsilon = 1e-05
momentum_decay = 0.9
outer_rate = 0.7

D = 4096
K = 512
B = 512
H = 256
NB = D // B
SCALE = float(D) ** (-0.5)
F32 = jnp.float32
BF16 = jnp.bfloat16
VMEM = pl.BlockSpec(memory_space=pltpu.VMEM)
SMEM = pl.BlockSpec(memory_space=pltpu.SMEM)
PARAMS = pltpu.CompilerParams(vmem_limit_bytes=40 << 20)


def columns(place, slot):
    return pl.ds(pl.multiple_of(place[slot] * B, B), B)


def norm_kernel(place, tok, gain, cot, normed, send, inverse):
    total = jnp.zeros((tok.shape[0], 1), F32)
    for j in range(NB):
        part = tok[:, j * B : (j + 1) * B].astype(F32)
        total += jnp.sum(part * part, axis=1, keepdims=True)
    scale = lax.rsqrt(total * (1.0 / D) + epsilon)
    inverse[...] = scale
    for j in range(NB):
        where = columns(place, j)
        value = (tok[:, where].astype(F32) * scale * gain[:, where].astype(F32)).astype(BF16)
        normed[j] = value
        if j >= 5:
            send[:, (7 - j) * B : (8 - j) * B] = value
    send[:, 3 * B : 4 * B] = cot[...]
    other = pl.multiple_of((1 - place[NB]) * H, H)
    send[:, 4 * B : 4 * B + H] = normed[4, :, pl.ds(other, H)]


def outer(a, b):
    return lax.dot_general(a, b, (((0,), (0,)), ((), ())), preferred_element_type=F32)


def grad_kernel(place, normed, cot, got, half, terms, own):
    mine = cot[...]
    theirs = got[:, 3 * B : 4 * B]
    here = pl.multiple_of(place[NB] * H, H)
    half[...] = (
        (outer(normed[4, :, pl.ds(here, H)], mine) + outer(got[:, 4 * B : 4 * B + H], theirs)) * SCALE
    ).astype(BF16)
    for j in (3, 2, 1):
        terms[j - 1] = (
            outer(normed[j], mine) + outer(got[:, (j - 1) * B : j * B], theirs)
        ) * SCALE
    own[...] = outer(normed[0], mine) * SCALE


def token_kernel(
    place, tok, gain, inverse, normed, cot, w0, w1, w2, w3, h4, swapped, swapped4, keys, grad, w4, back
):
    here = pl.multiple_of(place[NB] * H, H)
    there = pl.multiple_of((1 - place[NB]) * H, H)
    w4[pl.ds(here, H), :] = h4[...]
    w4[pl.ds(there, H), :] = swapped4[...]
    blocks = (w0, w1, w2, w3, w4, swapped.at[2], swapped.at[1], swapped.at[0])
    mine = cot[...]
    total = jnp.zeros(keys.shape, F32)
    mixed = jnp.zeros((tok.shape[0], 1), F32)
    for j, block in enumerate(blocks):
        where = columns(place, j)
        w = block[...]
        total += jnp.dot(normed[j], w, preferred_element_type=F32)
        down = (
            lax.dot_general(mine, w, (((1,), (1,)), ((), ())), preferred_element_type=F32) * SCALE
        ).astype(BF16)
        back[j] = down
        up = down.astype(F32) * gain[:, where].astype(F32)
        mixed += jnp.sum(up * tok[:, where].astype(F32), axis=1, keepdims=True)
    keys[...] = (total * SCALE).astype(BF16)
    scale = inverse[...]
    factor = scale * scale * (mixed * (1.0 / D))
    for j in range(NB):
        where = columns(place, j)
        up = back[j].astype(F32) * gain[:, where].astype(F32)
        grad[:, where] = (scale * (up - tok[:, where].astype(F32) * factor)).astype(BF16)


def shape(dims, kind):
    return jax.ShapeDtypeStruct(dims, kind)


def per_device(tokens, norm_gain, weight, momentum, key_grad, matching):
    rows = tokens.shape[0]
    n = 32
    me = lax.axis_index("fsdp")
    z, y, core = me // 4, (me // 2) % 2, me % 2
    sign = 2 * core - 1
    place = jnp.concatenate([(z + sign * jnp.arange(NB) + NB) % NB, core[None]]).astype(jnp.int32)
    gain = norm_gain[None]

    def along(v, perm):
        return lax.ppermute(v, "fsdp", perm)

    swap_core = [(i, i ^ 1) for i in range(n)]
    swap_y = [(i, i ^ 2) for i in range(n)]
    sums_on = [(i, (i + (4 if i % 2 else -4)) % n) for i in range(n)]
    rows_on = [(i, (i - (4 if i % 2 else -4)) % n) for i in range(n)]

    r = lax.axis_index("rep")
    rx, ry = r // 4, r % 4
    both = jnp.concatenate([weight[0], momentum[0]], axis=0)
    from_x = [both] + [
        lax.ppermute(both, "rep", [(i, (i + 4 * k) % 16) for i in range(16)]) for k in (1, 2, 3)
    ]

    def wanted_by(row):
        source = lax.dynamic_index_in_dim(matching, row, 0, keepdims=False)
        k = (rx - source // 4 + 4) % 4
        return lax.select_n(k, *from_x)

    local = weight[0]
    other_y = along(local, swap_y)
    pair = jnp.where(y == 0, jnp.stack([local, other_y]), jnp.stack([other_y, local]))
    other_pair = along(pair, swap_core)
    w0 = jnp.where(
        core == 0,
        jnp.stack([pair, other_pair], axis=1),
        jnp.stack([other_pair, pair], axis=1),
    ).reshape(B, K)

    normed, send, inverse = pl.pallas_call(
        norm_kernel,
        out_shape=(
            shape((NB, rows, B), BF16),
            shape((rows, 4 * B + H), BF16),
            shape((rows, 1), F32),
        ),
        in_specs=[SMEM, VMEM, VMEM, VMEM],
        out_specs=(VMEM, VMEM, VMEM),
        compiler_params=PARAMS,
        name="norm",
    )(place, tokens, gain, key_grad)
    got = along(send, swap_core)
    half, terms, own = pl.pallas_call(
        grad_kernel,
        out_shape=(shape((H, K), BF16), shape((3, B, K), F32), shape((B, K), F32)),
        in_specs=[SMEM, VMEM, VMEM, VMEM],
        out_specs=(VMEM, VMEM, VMEM),
        compiler_params=PARAMS,
        name="weight_grad",
    )(place, normed, key_grad, got)

    w1 = along(w0, rows_on)
    s3 = along(half, sums_on)
    w2 = along(w1, rows_on)
    s3 = s3.astype(F32)
    nothing = jnp.zeros_like(s3)
    s3 = jnp.where(
        core == 0, jnp.concatenate([s3, nothing], axis=0), jnp.concatenate([nothing, s3], axis=0)
    )
    s2 = along((terms[2] + s3).astype(BF16), sums_on)
    w3 = along(w2, rows_on)
    s1 = along((terms[1] + s2.astype(F32)).astype(BF16), sums_on)
    h4 = along(lax.dynamic_slice_in_dim(w3, core * H, H, 0), rows_on)
    s0 = along((terms[0] + s1.astype(F32)).astype(BF16), sums_on)
    swapped = along(jnp.stack([w1, w2, w3]), swap_core)
    swapped4 = along(h4, swap_core)

    keys, token_grad = pl.pallas_call(
        token_kernel,
        out_shape=(shape((rows, K), BF16), shape((rows, D), BF16)),
        in_specs=[SMEM] + [VMEM] * 12,
        out_specs=(VMEM, VMEM),
        scratch_shapes=[pltpu.VMEM((B, K), BF16), pltpu.VMEM((NB, rows, B), BF16)],
        compiler_params=PARAMS,
        name="token_grad",
    )(place, tokens, gain, inverse, normed, key_grad, w0, w1, w2, w3, h4, swapped, swapped4)

    total = (own + s0.astype(F32)).reshape(2, 2, B // 4, K)
    theirs = lax.dynamic_index_in_dim(total, 1 - core, 1, keepdims=False).astype(BF16)
    total = lax.dynamic_index_in_dim(total, core, 1, keepdims=False) + along(
        theirs, swap_core
    ).astype(F32)
    theirs = lax.dynamic_index_in_dim(total, 1 - y, 0, keepdims=False).astype(BF16)
    grad = lax.dynamic_index_in_dim(total, y, 0, keepdims=False) + along(theirs, swap_y).astype(F32)
    grad = grad.astype(BF16).astype(F32)

    from_y = [wanted_by(r)]
    for m in (1, 2, 3):
        target = rx * 4 + (ry + m) % 4
        from_y.append(
            lax.ppermute(
                wanted_by(target), "rep", [(i, i // 4 * 4 + (i + m) % 4) for i in range(16)]
            )
        )
    source = lax.dynamic_index_in_dim(matching, r, 0, keepdims=False)
    partner = lax.select_n((ry - source % 4 + 4) % 4, *from_y).astype(F32)
    mean = (both.astype(F32) + partner) * 0.5
    rows_w = weight.shape[1]
    mean_weight, mean_momentum = mean[:rows_w], mean[rows_w:]
    momentum_next = momentum_decay * mean_momentum + grad
    new_weight = (mean_weight - outer_rate * (grad + momentum_decay * momentum_next)).astype(BF16)
    return (keys, token_grad, new_weight[None], momentum_next.astype(BF16)[None])


def solution(mesh):
    in_specs = (
        P(("rep", "fsdp"), None),
        P(),
        P("rep", "fsdp", None),
        P("rep", "fsdp", None),
        P(("rep", "fsdp"), None),
        P(),
    )
    out_specs = (
        P(("rep", "fsdp"), None),
        P(("rep", "fsdp"), None),
        P("rep", "fsdp", None),
        P("rep", "fsdp", None),
    )
    return jax.shard_map(
        per_device, mesh=mesh, in_specs=in_specs, out_specs=out_specs, check_vma=False
    )
```

```python
import functools

import jax
import jax.numpy as jnp
from jax import lax
from jax.experimental import pallas as pl
from jax.experimental.pallas import tpu as pltpu
from jax.sharding import PartitionSpec as P

epsilon = 1e-05
momentum_decay = 0.9
outer_rate = 0.7

D = 4096
K = 512
B = 512
H = 256
NB = D // B
SCALE = float(D) ** (-0.5)
F32 = jnp.float32
BF16 = jnp.bfloat16
VMEM = pl.BlockSpec(memory_space=pltpu.VMEM)
SMEM = pl.BlockSpec(memory_space=pltpu.SMEM)
ANY = pl.BlockSpec(memory_space=pl.ANY)


def columns(place, slot):
    return pl.ds(pl.multiple_of(place[slot] * B, B), B)


def norm_kernel(place, tok, gain, cot, normed, send, inverse):
    total = jnp.zeros((tok.shape[0], 1), F32)
    for j in range(NB):
        part = tok[:, j * B : (j + 1) * B].astype(F32)
        total += jnp.sum(part * part, axis=1, keepdims=True)
    scale = lax.rsqrt(total * (1.0 / D) + epsilon)
    inverse[...] = scale
    for j in range(NB):
        where = columns(place, j)
        value = (tok[:, where].astype(F32) * scale * gain[:, where].astype(F32)).astype(BF16)
        normed[j] = value
        if j >= 5:
            send[:, (7 - j) * B : (8 - j) * B] = value
    send[:, 3 * B : 4 * B] = cot[...]
    other = pl.multiple_of((1 - place[NB]) * H, H)
    send[:, 4 * B : 4 * B + H] = normed[4, :, pl.ds(other, H)]


def outer(a, b):
    return lax.dot_general(a, b, (((0,), (0,)), ((), ())), preferred_element_type=F32)


def grad_kernel(place, normed, cot, got, half, term3, term2, term1, own):
    mine = cot[...]
    theirs = got[:, 3 * B : 4 * B]
    here = pl.multiple_of(place[NB] * H, H)
    half[...] = (
        (outer(normed[4, :, pl.ds(here, H)], mine) + outer(got[:, 4 * B : 4 * B + H], theirs)) * SCALE
    ).astype(BF16)
    for j, term in ((3, term3), (2, term2), (1, term1)):
        term[...] = (
            outer(normed[j], mine) + outer(got[:, (j - 1) * B : j * B], theirs)
        ) * SCALE
    own[...] = outer(normed[0], mine) * SCALE


def token_kernel(
    place, tok, gain, inverse, normed, cot, w0, w7, w6, w5, h4, swapped, swapped4, keys, grad, w4, back
):
    here = pl.multiple_of(place[NB] * H, H)
    there = pl.multiple_of((1 - place[NB]) * H, H)
    w4[pl.ds(here, H), :] = h4[...]
    w4[pl.ds(there, H), :] = swapped4[...]
    blocks = (w0, swapped.at[0], swapped.at[1], swapped.at[2], w4, w5, w6, w7)
    mine = cot[...]
    total = jnp.zeros(keys.shape, F32)
    mixed = jnp.zeros((tok.shape[0], 1), F32)
    for j, block in enumerate(blocks):
        where = columns(place, j)
        w = block[...]
        total += jnp.dot(normed[j], w, preferred_element_type=F32)
        down = (
            lax.dot_general(mine, w, (((1,), (1,)), ((), ())), preferred_element_type=F32) * SCALE
        ).astype(BF16)
        back[j] = down
        up = down.astype(F32) * gain[:, where].astype(F32)
        mixed += jnp.sum(up * tok[:, where].astype(F32), axis=1, keepdims=True)
    keys[...] = (total * SCALE).astype(BF16)
    scale = inverse[...]
    factor = scale * scale * (mixed * (1.0 / D))
    for j in range(NB):
        where = columns(place, j)
        up = back[j].astype(F32) * gain[:, where].astype(F32)
        grad[:, where] = (scale * (up - tok[:, where].astype(F32) * factor)).astype(BF16)


def join_kernel(place, local, other_y, other_core, rows):
    core, y = place[NB], place[NB + 1]
    rows[2 * y + core] = local[0]
    rows[2 * (1 - y) + core] = other_y[0]
    rows[2 * y + 1 - core] = other_core[0]
    rows[2 * (1 - y) + 1 - core] = other_core[1]


def first_sum_kernel(place, term, got, earlier, total):
    here = pl.ds(pl.multiple_of(place[NB] * H, H), H)
    total[...] = term[...].astype(BF16)
    total[here, :] = (term[here, :] + got[...].astype(F32)).astype(BF16)


def sum_kernel(term, got, earlier, total):
    total[...] = (term[...] + got[...].astype(F32)).astype(BF16)


def core_kernel(place, own, got, keep, give):
    core = place[NB]
    for y in range(2):
        mine, theirs = 2 * y + core, 2 * y + 1 - core
        keep[y] = own[mine] + got[mine].astype(F32)
        give[y] = (own[theirs] + got[theirs].astype(F32)).astype(BF16)


def y_kernel(place, kept, got, keep, give):
    y = place[NB + 1]
    keep[...] = kept[y] + got[y].astype(F32)
    give[0] = (kept[1 - y] + got[1 - y].astype(F32)).astype(BF16)


def choose_kernel(matching, pieces, chosen):
    for d in range(pieces.shape[0]):
        chosen[d] = pieces[matching[d]]


def update_kernel(kept, got, weight, momentum, partner, new_weight, new_momentum):
    n = kept.shape[0]
    grad = (kept[...] + got[0].astype(F32)).astype(BF16).astype(F32)
    mean_weight = (weight[0].astype(F32) + partner[:n].astype(F32)) * 0.5
    mean_momentum = (momentum[0].astype(F32) + partner[n:].astype(F32)) * 0.5
    following = momentum_decay * mean_momentum + grad
    new_momentum[0] = following.astype(BF16)
    new_weight[0] = (mean_weight - outer_rate * (grad + momentum_decay * following)).astype(BF16)


def shape(dims, kind):
    return jax.ShapeDtypeStruct(dims, kind)


def call(kernel, name, out, specs, *args, scratch=(), vmem=12):
    single = not isinstance(out, tuple)
    return pl.pallas_call(
        kernel,
        out_shape=out,
        in_specs=specs,
        out_specs=VMEM if single else (VMEM,) * len(out),
        scratch_shapes=scratch,
        compiler_params=pltpu.CompilerParams(vmem_limit_bytes=vmem << 20),
        name=name,
    )(*args)


def per_device(tokens, norm_gain, weight, momentum, key_grad, matching):
    rows = tokens.shape[0]
    part = weight.shape[1]
    n = 32
    lane = jnp.arange(16, dtype=jnp.int32)
    me = jnp.full((16,), lax.axis_index("fsdp"), jnp.int32)
    group = jnp.full((16,), lax.axis_index("rep"), jnp.int32)
    core = me & 1
    place = jnp.where(lane < NB, ((me >> 2) + (2 * core - 1) * lane) & (NB - 1), group & 3)
    place = jnp.where(lane == NB, core, place)
    place = jnp.where(lane == NB + 1, (me >> 1) & 1, place)
    place = jnp.where(lane == NB + 2, group >> 2, place)
    gain = norm_gain[None]

    def along(v, perm):
        return lax.ppermute(v, "fsdp", perm)

    def after(v, *others):
        return lax.optimization_barrier((v, *others))

    swap_core = [(i, i ^ 1) for i in range(n)]
    swap_y = [(i, i ^ 2) for i in range(n)]
    on = [(i, (i + (4 if i % 2 else -4)) % n) for i in range(n)]

    def exchange(v):
        return lax.all_to_all(v, "rep", 0, 0)

    other_y = along(weight, swap_y)

    normed, send, inverse = call(
        norm_kernel,
        "norm",
        (shape((NB, rows, B), BF16), shape((rows, 4 * B + H), BF16), shape((rows, 1), F32)),
        [SMEM, VMEM, VMEM, VMEM],
        place,
        tokens,
        gain,
        key_grad,
    )
    both = jnp.concatenate([after(weight, inverse)[0][0], momentum[0]], axis=0)
    both = both.reshape(16, part // 8, K)
    send, other_y = after(send, other_y)
    got = along(send, swap_core)
    other_core = along(jnp.concatenate([weight, other_y], axis=0), swap_core)
    w0 = call(
        join_kernel,
        "join",
        shape((4, part, K), BF16),
        [SMEM, VMEM, VMEM, VMEM],
        place,
        weight,
        other_y,
        other_core,
    ).reshape(B, K)
    got = after(got, w0)[0]
    half, term3, term2, term1, own = call(
        grad_kernel,
        "weight_grad",
        (shape((H, K), BF16),) + (shape((B, K), F32),) * 4,
        [SMEM, VMEM, VMEM, VMEM],
        place,
        normed,
        key_grad,
        got,
    )

    block = shape((B, K), BF16)
    sums = [VMEM, VMEM, ANY]
    w7 = along(w0, on)
    s3 = along(half, on)
    w7 = after(w7, s3)[0]
    w6 = along(w7, on)
    p3 = call(first_sum_kernel, "sum_3", block, [SMEM] + sums, place, term3, s3, w7)
    s2 = along(p3, on)
    pieces = exchange(after(both, p3)[0])
    p2 = call(sum_kernel, "sum_2", block, sums, term2, s2, p3)
    w6 = after(w6, p2)[0]
    w5 = along(w6, on)
    s1 = along(p2, on)
    chosen = call(
        choose_kernel, "choose", shape(both.shape, BF16), [SMEM, VMEM], matching, pieces
    )
    p1 = call(sum_kernel, "sum_1", block, sums, term1, s1, chosen)
    w5 = after(w5, p1)[0]
    partner = exchange(after(chosen, p1)[0])
    core_here = lax.axis_index("fsdp") & 1
    h4 = along(lax.dynamic_slice_in_dim(w5, core_here * H, H, 0), on)
    partner = partner.reshape(2 * part, K)
    s0 = along(p1, on)
    swapped = along(jnp.stack([w7, w6, w5]), swap_core)
    swapped4 = along(h4, swap_core)

    kept, give = call(
        core_kernel,
        "core_sum",
        (shape((2, part, K), F32), shape((2, part, K), BF16)),
        [SMEM, VMEM, VMEM],
        place,
        own.reshape(4, part, K),
        s0.reshape(4, part, K),
    )
    got = along(give, swap_core)
    kept, give = call(
        y_kernel,
        "y_sum",
        (shape((part, K), F32), shape((1, part, K), BF16)),
        [SMEM, VMEM, VMEM],
        place,
        kept,
        got,
    )
    give, swapped4 = after(give, swapped4)
    got = along(give, swap_y)

    keys, token_grad = call(
        token_kernel,
        "token_grad",
        (shape((rows, K), BF16), shape((rows, D), BF16)),
        [SMEM] + [VMEM] * 12,
        place,
        tokens,
        gain,
        inverse,
        normed,
        key_grad,
        w0,
        w7,
        w6,
        w5,
        h4,
        swapped,
        swapped4,
        scratch=[pltpu.VMEM((B, K), BF16), pltpu.VMEM((NB, rows, B), BF16)],
        vmem=24,
    )
    keys, token_grad, got = after(keys, token_grad, got)
    new_weight, new_momentum = call(
        update_kernel,
        "update",
        (shape((1, part, K), BF16), shape((1, part, K), BF16)),
        [VMEM] * 5,
        kept,
        got,
        weight,
        momentum,
        partner,
        vmem=40,
    )
    return (keys, token_grad, new_weight, new_momentum)


def solution(mesh):
    in_specs = (
        P(("rep", "fsdp"), None),
        P(),
        P("rep", "fsdp", None),
        P("rep", "fsdp", None),
        P(("rep", "fsdp"), None),
        P(),
    )
    out_specs = (
        P(("rep", "fsdp"), None),
        P(("rep", "fsdp"), None),
        P("rep", "fsdp", None),
        P("rep", "fsdp", None),
    )
    return jax.shard_map(
        per_device, mesh=mesh, in_specs=in_specs, out_specs=out_specs, check_vma=False
    )
```

```python
import functools

import jax
import jax.numpy as jnp
from jax import lax
from jax.experimental import pallas as pl
from jax.experimental.pallas import tpu as pltpu
from jax.sharding import PartitionSpec as P

epsilon = 1e-05
momentum_decay = 0.9
outer_rate = 0.7

D = 4096
K = 512
B = 512
H = 256
NB = D // B
SCALE = float(D) ** (-0.5)
F32 = jnp.float32
BF16 = jnp.bfloat16
VMEM = pl.BlockSpec(memory_space=pltpu.VMEM)
SMEM = pl.BlockSpec(memory_space=pltpu.SMEM)
ANY = pl.BlockSpec(memory_space=pl.ANY)


def columns(place, slot):
    return pl.ds(pl.multiple_of(place[slot] * B, B), B)


def norm_kernel(place, tok_in, gain, cot, normed, send, inverse, tok, sems):
    count = tok.shape[0]
    chunk = 80 if count % 80 == 0 else count
    starts = range(0, count, chunk)
    loads = [
        pltpu.make_async_copy(
            tok_in.at[pl.ds(a, chunk)], tok.at[pl.ds(a, chunk)], sems.at[a // chunk]
        )
        for a in starts
    ]
    loads.append(pltpu.make_async_copy(cot, send.at[:, pl.ds(3 * B, B)], sems.at[len(starts)]))
    for load in loads:
        load.start()
    for a, load in zip(starts, loads):
        load.wait()
        rows = slice(a, a + chunk)
        total = jnp.zeros((chunk, 1), F32)
        for j in range(NB):
            part = tok[rows, j * B : (j + 1) * B].astype(F32)
            total += jnp.sum(part * part, axis=1, keepdims=True)
        scale = lax.rsqrt(total * (1.0 / D) + epsilon)
        inverse[rows, :] = scale
        for j in range(NB):
            where = columns(place, j)
            value = (tok[rows, where].astype(F32) * scale * gain[:, where].astype(F32)).astype(
                BF16
            )
            normed[j, rows, :] = value
            if j >= 5:
                send[rows, (7 - j) * B : (8 - j) * B] = value
    loads[-1].wait()
    other = pl.multiple_of((1 - place[NB]) * H, H)
    send[:, 4 * B : 4 * B + H] = normed[4, :, pl.ds(other, H)]


def outer(a, b):
    return lax.dot_general(a, b, (((0,), (0,)), ((), ())), preferred_element_type=F32)


def grad_kernel(place, normed, cot, got, half, term3, term2, term1, own):
    mine = cot[...]
    theirs = got[:, 3 * B : 4 * B]
    here = pl.multiple_of(place[NB] * H, H)
    half[...] = (
        (outer(normed[4, :, pl.ds(here, H)], mine) + outer(got[:, 4 * B : 4 * B + H], theirs)) * SCALE
    ).astype(BF16)
    for j, term in ((3, term3), (2, term2), (1, term1)):
        term[...] = (
            outer(normed[j], mine) + outer(got[:, (j - 1) * B : j * B], theirs)
        ) * SCALE
    own[...] = outer(normed[0], mine) * SCALE


def token_kernel(
    place, tok, gain, inverse, normed, cot, w0, w7, w6, w5, h4, swapped, swapped4, keys, grad, w4, back
):
    here = pl.multiple_of(place[NB] * H, H)
    there = pl.multiple_of((1 - place[NB]) * H, H)
    w4[pl.ds(here, H), :] = h4[...]
    w4[pl.ds(there, H), :] = swapped4[...]
    blocks = (w0, swapped.at[0], swapped.at[1], swapped.at[2], w4, w5, w6, w7)
    mine = cot[...]
    total = jnp.zeros(keys.shape, F32)
    mixed = jnp.zeros((tok.shape[0], 1), F32)
    for j, block in enumerate(blocks):
        where = columns(place, j)
        w = block[...]
        total += jnp.dot(normed[j], w, preferred_element_type=F32)
        down = (
            lax.dot_general(mine, w, (((1,), (1,)), ((), ())), preferred_element_type=F32) * SCALE
        ).astype(BF16)
        back[j] = down
        up = down.astype(F32) * gain[:, where].astype(F32)
        mixed += jnp.sum(up * tok[:, where].astype(F32), axis=1, keepdims=True)
    keys[...] = (total * SCALE).astype(BF16)
    scale = inverse[...]
    factor = scale * scale * (mixed * (1.0 / D))
    for j in range(NB):
        where = columns(place, j)
        up = back[j].astype(F32) * gain[:, where].astype(F32)
        grad[:, where] = (scale * (up - tok[:, where].astype(F32) * factor)).astype(BF16)


def join_kernel(place, local, other_y, other_core, rows):
    core, y = place[NB], place[NB + 1]
    rows[2 * y + core] = local[0]
    rows[2 * (1 - y) + core] = other_y[0]
    rows[2 * y + 1 - core] = other_core[0]
    rows[2 * (1 - y) + 1 - core] = other_core[1]


def first_sum_kernel(place, term, got, earlier, total):
    here = pl.ds(pl.multiple_of(place[NB] * H, H), H)
    total[...] = term[...].astype(BF16)
    total[here, :] = (term[here, :] + got[...].astype(F32)).astype(BF16)


def sum_kernel(term, got, earlier, total):
    total[...] = (term[...] + got[...].astype(F32)).astype(BF16)


def core_kernel(place, own, got, keep, give):
    core = place[NB]
    for y in range(2):
        mine, theirs = 2 * y + core, 2 * y + 1 - core
        keep[y] = own[mine] + got[mine].astype(F32)
        give[y] = (own[theirs] + got[theirs].astype(F32)).astype(BF16)


def y_kernel(place, kept, got, keep, give):
    y = place[NB + 1]
    keep[...] = kept[y] + got[y].astype(F32)
    give[0] = (kept[1 - y] + got[1 - y].astype(F32)).astype(BF16)


def choose_kernel(matching, pieces, chosen):
    for d in range(pieces.shape[0]):
        chosen[d] = pieces[matching[d]]


def update_kernel(kept, got, weight, momentum, partner, new_weight, new_momentum):
    n = kept.shape[0]
    grad = (kept[...] + got[0].astype(F32)).astype(BF16).astype(F32)
    mean_weight = (weight[0].astype(F32) + partner[:n].astype(F32)) * 0.5
    mean_momentum = (momentum[0].astype(F32) + partner[n:].astype(F32)) * 0.5
    following = momentum_decay * mean_momentum + grad
    new_momentum[0] = following.astype(BF16)
    new_weight[0] = (mean_weight - outer_rate * (grad + momentum_decay * following)).astype(BF16)


def shape(dims, kind):
    return jax.ShapeDtypeStruct(dims, kind)


def call(kernel, name, out, specs, *args, scratch=(), vmem=12):
    single = not isinstance(out, tuple)
    return pl.pallas_call(
        kernel,
        out_shape=out,
        in_specs=specs,
        out_specs=VMEM if single else (VMEM,) * len(out),
        scratch_shapes=scratch,
        compiler_params=pltpu.CompilerParams(vmem_limit_bytes=vmem << 20),
        name=name,
    )(*args)


def per_device(tokens, norm_gain, weight, momentum, key_grad, matching):
    rows = tokens.shape[0]
    part = weight.shape[1]
    n = 32
    lane = jnp.arange(16, dtype=jnp.int32)
    me = jnp.full((16,), lax.axis_index("fsdp"), jnp.int32)
    group = jnp.full((16,), lax.axis_index("rep"), jnp.int32)
    core = me & 1
    place = jnp.where(lane < NB, ((me >> 2) + (2 * core - 1) * lane) & (NB - 1), group & 3)
    place = jnp.where(lane == NB, core, place)
    place = jnp.where(lane == NB + 1, (me >> 1) & 1, place)
    place = jnp.where(lane == NB + 2, group >> 2, place)
    gain = norm_gain[None]

    def along(v, perm):
        return lax.ppermute(v, "fsdp", perm)

    def after(v, *others):
        return lax.optimization_barrier((v, *others))

    swap_core = [(i, i ^ 1) for i in range(n)]
    swap_y = [(i, i ^ 2) for i in range(n)]
    on = [(i, (i + (4 if i % 2 else -4)) % n) for i in range(n)]

    def exchange(v):
        return lax.all_to_all(v, "rep", 0, 0)

    other_y = along(weight, swap_y)

    normed, send, inverse = call(
        norm_kernel,
        "norm",
        (shape((NB, rows, B), BF16), shape((rows, 4 * B + H), BF16), shape((rows, 1), F32)),
        [SMEM, ANY, VMEM, ANY],
        place,
        tokens,
        gain,
        key_grad,
        scratch=[pltpu.VMEM((rows, D), BF16), pltpu.SemaphoreType.DMA((4,))],
        vmem=56,
    )
    both = jnp.concatenate([after(weight, inverse)[0][0], momentum[0]], axis=0)
    both = both.reshape(16, part // 8, K)
    send, other_y = after(send, other_y)
    got = along(send, swap_core)
    other_core = along(jnp.concatenate([weight, other_y], axis=0), swap_core)
    w0 = call(
        join_kernel,
        "join",
        shape((4, part, K), BF16),
        [SMEM, VMEM, VMEM, VMEM],
        place,
        weight,
        other_y,
        other_core,
    ).reshape(B, K)
    got = after(got, w0)[0]
    half, term3, term2, term1, own = call(
        grad_kernel,
        "weight_grad",
        (shape((H, K), BF16),) + (shape((B, K), F32),) * 4,
        [SMEM, VMEM, VMEM, VMEM],
        place,
        normed,
        key_grad,
        got,
    )

    block = shape((B, K), BF16)
    sums = [VMEM, VMEM, ANY]
    w7 = along(w0, on)
    s3 = along(half, on)
    w7 = after(w7, s3)[0]
    w6 = along(w7, on)
    p3 = call(first_sum_kernel, "sum_3", block, [SMEM] + sums, place, term3, s3, w7)
    s2 = along(p3, on)
    pieces = exchange(after(both, p3)[0])
    p2 = call(sum_kernel, "sum_2", block, sums, term2, s2, p3)
    w6 = after(w6, p2)[0]
    w5 = along(w6, on)
    s1 = along(p2, on)
    chosen = call(
        choose_kernel, "choose", shape(both.shape, BF16), [SMEM, VMEM], matching, pieces
    )
    p1 = call(sum_kernel, "sum_1", block, sums, term1, s1, chosen)
    w5 = after(w5, p1)[0]
    partner = exchange(after(chosen, p1)[0])
    core_here = lax.axis_index("fsdp") & 1
    h4 = along(lax.dynamic_slice_in_dim(w5, core_here * H, H, 0), on)
    partner = partner.reshape(2 * part, K)
    s0 = along(p1, on)
    swapped = along(jnp.stack([w7, w6, w5]), swap_core)
    swapped4 = along(h4, swap_core)

    kept, give = call(
        core_kernel,
        "core_sum",
        (shape((2, part, K), F32), shape((2, part, K), BF16)),
        [SMEM, VMEM, VMEM],
        place,
        own.reshape(4, part, K),
        s0.reshape(4, part, K),
    )
    got = along(give, swap_core)
    kept, give = call(
        y_kernel,
        "y_sum",
        (shape((part, K), F32), shape((1, part, K), BF16)),
        [SMEM, VMEM, VMEM],
        place,
        kept,
        got,
    )
    give, swapped4 = after(give, swapped4)
    got = along(give, swap_y)

    keys, token_grad = call(
        token_kernel,
        "token_grad",
        (shape((rows, K), BF16), shape((rows, D), BF16)),
        [SMEM] + [VMEM] * 12,
        place,
        tokens,
        gain,
        inverse,
        normed,
        key_grad,
        w0,
        w7,
        w6,
        w5,
        h4,
        swapped,
        swapped4,
        scratch=[pltpu.VMEM((B, K), BF16), pltpu.VMEM((NB, rows, B), BF16)],
        vmem=56,
    )
    keys, token_grad, got = after(keys, token_grad, got)
    new_weight, new_momentum = call(
        update_kernel,
        "update",
        (shape((1, part, K), BF16), shape((1, part, K), BF16)),
        [VMEM] * 5,
        kept,
        got,
        weight,
        momentum,
        partner,
        vmem=40,
    )
    return (keys, token_grad, new_weight, new_momentum)


def solution(mesh):
    in_specs = (
        P(("rep", "fsdp"), None),
        P(),
        P("rep", "fsdp", None),
        P("rep", "fsdp", None),
        P(("rep", "fsdp"), None),
        P(),
    )
    out_specs = (
        P(("rep", "fsdp"), None),
        P(("rep", "fsdp"), None),
        P("rep", "fsdp", None),
        P("rep", "fsdp", None),
    )
    return jax.shard_map(
        per_device, mesh=mesh, in_specs=in_specs, out_specs=out_specs, check_vma=False
    )
```

```python
import functools

import jax
import jax.numpy as jnp
from jax import lax
from jax.experimental import pallas as pl
from jax.experimental.pallas import tpu as pltpu
from jax.sharding import PartitionSpec as P

epsilon = 1e-05
momentum_decay = 0.9
outer_rate = 0.7

D = 4096
K = 512
B = 512
H = 256
NB = D // B
SCALE = float(D) ** (-0.5)
F32 = jnp.float32
BF16 = jnp.bfloat16
VMEM = pl.BlockSpec(memory_space=pltpu.VMEM)
SMEM = pl.BlockSpec(memory_space=pltpu.SMEM)
ANY = pl.BlockSpec(memory_space=pl.ANY)


def columns(place, slot):
    return pl.ds(pl.multiple_of(place[slot] * B, B), B)


def norm_kernel(place, tok_in, gain_in, cot, normed, send, inverse, tok, gain, sems):
    gain[...] = gain_in[...].astype(F32).reshape(gain.shape)
    count = tok.shape[0]
    chunk = 80 if count % 80 == 0 else count
    starts = range(0, count, chunk)
    loads = [
        pltpu.make_async_copy(
            tok_in.at[pl.ds(a, chunk)], tok.at[pl.ds(a, chunk)], sems.at[a // chunk]
        )
        for a in starts
    ]
    loads.append(pltpu.make_async_copy(cot, send.at[:, pl.ds(3 * B, B)], sems.at[len(starts)]))
    for load in loads:
        load.start()
    for a, load in zip(starts, loads):
        load.wait()
        rows = slice(a, a + chunk)
        total = jnp.zeros((chunk, 1), F32)
        for j in range(NB):
            part = tok[rows, j * B : (j + 1) * B].astype(F32)
            total += jnp.sum(part * part, axis=1, keepdims=True)
        scale = lax.rsqrt(total * (1.0 / D) + epsilon)
        inverse[rows, :] = scale
        for j in range(NB):
            where = columns(place, j)
            value = (tok[rows, where].astype(F32) * scale * gain[:, where]).astype(
                BF16
            )
            normed[j, rows, :] = value
            if j >= 5:
                send[rows, (7 - j) * B : (8 - j) * B] = value
    loads[-1].wait()
    other = pl.multiple_of((1 - place[NB]) * H, H)
    send[:, 4 * B : 4 * B + H] = normed[4, :, pl.ds(other, H)]


def outer(a, b):
    return lax.dot_general(a, b, (((0,), (0,)), ((), ())), preferred_element_type=F32)


def grad_kernel(place, normed, cot, got, half, term3, term2, term1, own):
    mine = cot[...]
    theirs = got[:, 3 * B : 4 * B]
    here = pl.multiple_of(place[NB] * H, H)
    half[...] = (
        (outer(normed[4, :, pl.ds(here, H)], mine) + outer(got[:, 4 * B : 4 * B + H], theirs)) * SCALE
    ).astype(BF16)
    for j, term in ((3, term3), (2, term2), (1, term1)):
        term[...] = (
            outer(normed[j], mine) + outer(got[:, (j - 1) * B : j * B], theirs)
        ) * SCALE
    own[...] = outer(normed[0], mine) * SCALE


def token_kernel(
    place, tok_in, gain_in, inverse, normed_in, cot, w0, w7, w6, w5, h4, swapped, swapped4,
    keys, grad, w4, back, tok, normed, gain, sems,
):
    gain[...] = gain_in[...].astype(F32).reshape(gain.shape)
    load_normed = pltpu.make_async_copy(normed_in, normed, sems.at[0])
    load_tok = pltpu.make_async_copy(tok_in, tok, sems.at[1])
    load_normed.start()
    load_tok.start()
    here = pl.multiple_of(place[NB] * H, H)
    there = pl.multiple_of((1 - place[NB]) * H, H)
    w4[pl.ds(here, H), :] = h4[...]
    w4[pl.ds(there, H), :] = swapped4[...]
    blocks = (w0, swapped.at[0], swapped.at[1], swapped.at[2], w4, w5, w6, w7)
    mine = cot[...]
    for j, block in enumerate(blocks):
        back[j] = (
            lax.dot_general(mine, block[...], (((1,), (1,)), ((), ())), preferred_element_type=F32)
            * SCALE
        ).astype(BF16)
    load_normed.wait()
    total = jnp.zeros(keys.shape, F32)
    for j, block in enumerate(blocks):
        total += jnp.dot(normed[j], block[...], preferred_element_type=F32)
    keys[...] = (total * SCALE).astype(BF16)
    load_tok.wait()
    mixed = jnp.zeros((tok.shape[0], 1), F32)
    for j in range(NB):
        where = columns(place, j)
        up = back[j].astype(F32) * gain[:, where]
        mixed += jnp.sum(up * tok[:, where].astype(F32), axis=1, keepdims=True)
    scale = inverse[...]
    factor = scale * scale * (mixed * (1.0 / D))
    for j in range(NB):
        where = columns(place, j)
        up = back[j].astype(F32) * gain[:, where]
        grad[:, where] = (scale * (up - tok[:, where].astype(F32) * factor)).astype(BF16)


def join_kernel(place, local, other_y, other_core, rows):
    core, y = place[NB], place[NB + 1]
    rows[2 * y + core] = local[0]
    rows[2 * (1 - y) + core] = other_y[0]
    rows[2 * y + 1 - core] = other_core[0]
    rows[2 * (1 - y) + 1 - core] = other_core[1]


def first_sum_kernel(place, term, got, earlier, total):
    here = pl.ds(pl.multiple_of(place[NB] * H, H), H)
    total[...] = term[...].astype(BF16)
    total[here, :] = (term[here, :] + got[...].astype(F32)).astype(BF16)


def sum_kernel(term, got, earlier, total):
    total[...] = (term[...] + got[...].astype(F32)).astype(BF16)


def core_kernel(place, own, got, keep, give):
    core = place[NB]
    for y in range(2):
        mine, theirs = 2 * y + core, 2 * y + 1 - core
        keep[y] = own[mine] + got[mine].astype(F32)
        give[y] = (own[theirs] + got[theirs].astype(F32)).astype(BF16)


def y_kernel(place, kept, got, keep, give):
    y = place[NB + 1]
    keep[...] = kept[y] + got[y].astype(F32)
    give[0] = (kept[1 - y] + got[1 - y].astype(F32)).astype(BF16)


def choose_kernel(matching, pieces, chosen):
    for d in range(pieces.shape[0]):
        chosen[d] = pieces[matching[d]]


def update_kernel(kept, got, weight, momentum, partner, new_weight, new_momentum):
    n = kept.shape[0]
    grad = (kept[...] + got[0].astype(F32)).astype(BF16).astype(F32)
    mean_weight = (weight[0].astype(F32) + partner[:n].astype(F32)) * 0.5
    mean_momentum = (momentum[0].astype(F32) + partner[n:].astype(F32)) * 0.5
    following = momentum_decay * mean_momentum + grad
    new_momentum[0] = following.astype(BF16)
    new_weight[0] = (mean_weight - outer_rate * (grad + momentum_decay * following)).astype(BF16)


def shape(dims, kind):
    return jax.ShapeDtypeStruct(dims, kind)


def call(kernel, name, out, specs, *args, scratch=(), vmem=12):
    single = not isinstance(out, tuple)
    return pl.pallas_call(
        kernel,
        out_shape=out,
        in_specs=specs,
        out_specs=VMEM if single else (VMEM,) * len(out),
        scratch_shapes=scratch,
        compiler_params=pltpu.CompilerParams(vmem_limit_bytes=vmem << 20),
        name=name,
    )(*args)


def per_device(tokens, norm_gain, weight, momentum, key_grad, matching):
    rows = tokens.shape[0]
    part = weight.shape[1]
    n = 32
    lane = jnp.arange(16, dtype=jnp.int32)
    me = jnp.full((16,), lax.axis_index("fsdp"), jnp.int32)
    group = jnp.full((16,), lax.axis_index("rep"), jnp.int32)
    core = me & 1
    place = jnp.where(lane < NB, ((me >> 2) + (2 * core - 1) * lane) & (NB - 1), group & 3)
    place = jnp.where(lane == NB, core, place)
    place = jnp.where(lane == NB + 1, (me >> 1) & 1, place)
    place = jnp.where(lane == NB + 2, group >> 2, place)
    gain = norm_gain

    def along(v, perm):
        return lax.ppermute(v, "fsdp", perm)

    def after(v, *others):
        return lax.optimization_barrier((v, *others))

    swap_core = [(i, i ^ 1) for i in range(n)]
    swap_y = [(i, i ^ 2) for i in range(n)]
    on = [(i, (i + (4 if i % 2 else -4)) % n) for i in range(n)]

    def exchange(v):
        return lax.all_to_all(v, "rep", 0, 0)

    other_y = along(weight, swap_y)

    normed, send, inverse = call(
        norm_kernel,
        "norm",
        (shape((NB, rows, B), BF16), shape((rows, 4 * B + H), BF16), shape((rows, 1), F32)),
        [SMEM, ANY, VMEM, ANY],
        place,
        tokens,
        gain,
        key_grad,
        scratch=[
            pltpu.VMEM((rows, D), BF16),
            pltpu.VMEM((1, D), F32),
            pltpu.SemaphoreType.DMA((4,)),
        ],
        vmem=56,
    )
    both = jnp.concatenate([after(weight, inverse)[0][0], momentum[0]], axis=0)
    both = both.reshape(16, part // 8, K)
    send, other_y = after(send, other_y)
    got = along(send, swap_core)
    other_core = along(jnp.concatenate([weight, other_y], axis=0), swap_core)
    w0 = call(
        join_kernel,
        "join",
        shape((4, part, K), BF16),
        [SMEM, VMEM, VMEM, VMEM],
        place,
        weight,
        other_y,
        other_core,
    ).reshape(B, K)
    got = after(got, w0)[0]
    half, term3, term2, term1, own = call(
        grad_kernel,
        "weight_grad",
        (shape((H, K), BF16),) + (shape((B, K), F32),) * 4,
        [SMEM, VMEM, VMEM, VMEM],
        place,
        normed,
        key_grad,
        got,
    )

    block = shape((B, K), BF16)
    sums = [VMEM, VMEM, ANY]
    w7 = along(w0, on)
    s3 = along(half, on)
    w7 = after(w7, s3)[0]
    w6 = along(w7, on)
    p3 = call(first_sum_kernel, "sum_3", block, [SMEM] + sums, place, term3, s3, w7)
    s2 = along(p3, on)
    pieces = exchange(after(both, p3)[0])
    p2 = call(sum_kernel, "sum_2", block, sums, term2, s2, p3)
    w6 = after(w6, p2)[0]
    w5 = along(w6, on)
    s1 = along(p2, on)
    chosen = call(
        choose_kernel, "choose", shape(both.shape, BF16), [SMEM, VMEM], matching, pieces
    )
    p1 = call(sum_kernel, "sum_1", block, sums, term1, s1, chosen)
    w5 = after(w5, p1)[0]
    partner = exchange(after(chosen, p1)[0])
    core_here = lax.axis_index("fsdp") & 1
    h4 = along(lax.dynamic_slice_in_dim(w5, core_here * H, H, 0), on)
    partner = partner.reshape(2 * part, K)
    s0 = along(p1, on)
    swapped = along(jnp.stack([w7, w6, w5]), swap_core)
    swapped4 = along(h4, swap_core)

    kept, give = call(
        core_kernel,
        "core_sum",
        (shape((2, part, K), F32), shape((2, part, K), BF16)),
        [SMEM, VMEM, VMEM],
        place,
        own.reshape(4, part, K),
        s0.reshape(4, part, K),
    )
    got = along(give, swap_core)
    kept, give = call(
        y_kernel,
        "y_sum",
        (shape((part, K), F32), shape((1, part, K), BF16)),
        [SMEM, VMEM, VMEM],
        place,
        kept,
        got,
    )
    give, swapped4 = after(give, swapped4)
    got = along(give, swap_y)

    keys, token_grad = call(
        token_kernel,
        "token_grad",
        (shape((rows, K), BF16), shape((rows, D), BF16)),
        [SMEM, ANY, VMEM, VMEM, ANY] + [VMEM] * 8,
        place,
        tokens,
        gain,
        inverse,
        normed,
        key_grad,
        w0,
        w7,
        w6,
        w5,
        h4,
        swapped,
        swapped4,
        scratch=[
            pltpu.VMEM((B, K), BF16),
            pltpu.VMEM((NB, rows, B), BF16),
            pltpu.VMEM((rows, D), BF16),
            pltpu.VMEM((NB, rows, B), BF16),
            pltpu.VMEM((1, D), F32),
            pltpu.SemaphoreType.DMA((2,)),
        ],
        vmem=56,
    )
    keys, token_grad, got = after(keys, token_grad, got)
    new_weight, new_momentum = call(
        update_kernel,
        "update",
        (shape((1, part, K), BF16), shape((1, part, K), BF16)),
        [VMEM] * 5,
        kept,
        got,
        weight,
        momentum,
        partner,
        vmem=40,
    )
    return (keys, token_grad, new_weight, new_momentum)


def solution(mesh):
    in_specs = (
        P(("rep", "fsdp"), None),
        P(),
        P("rep", "fsdp", None),
        P("rep", "fsdp", None),
        P(("rep", "fsdp"), None),
        P(),
    )
    out_specs = (
        P(("rep", "fsdp"), None),
        P(("rep", "fsdp"), None),
        P("rep", "fsdp", None),
        P("rep", "fsdp", None),
    )
    return jax.shard_map(
        per_device, mesh=mesh, in_specs=in_specs, out_specs=out_specs, check_vma=False
    )
```
